512 devices in a mesh: inner: 16 (over z_hi, x, core), outer: 32 (over y, z_lo).
Axes of the slice: x: 4, y: 4, z: 16 (z_hi: 2, z_lo: 8; z = z_hi * 8 + z_lo), core: 2. Of those that a mesh axis runs over, the one named last changes fastest.
Arguments:
- queries: bfloat16 [65536, 1024], P(('inner', 'outer')), may hold values from -6 to 6
- keys: bfloat16 [65536, 128], P(('inner', 'outer')), may hold values from -6 to 6
- values: bfloat16 [65536, 128], P(('inner', 'outer')), may hold values from -6 to 6
- lengths: int32 [16], replicated, may hold values from 1 to 16384, 65536 in all
Outputs:
- attended: bfloat16 [65536, 1024], P(('inner', 'outer'))
The draws below stay inside these ranges and needn't reach their ends.
Inputs may be any that keep to these rules, and one draw needn't show every extreme that they name: lengths sum to 65536; the longest is exactly 16384.
All inputs are finite; a program needn't handle non-finite values.
Results may differ from the reference program's by a relative error of at most 0.0085.
Values may be sent and summed in bfloat16 or wider, within the bound.
No kernel may reach another device: no remote copies, remote signals or barrier semaphores. Data moves between devices by JAX's collectives and lax.ppermute only.
A program may use at most 64 MiB of HBM per device.

```python
import math
import jax
import jax.numpy as jnp
import numpy as np
from jax import lax

HEADS = 8
HEAD = 128
DOCS = 16
SEQ = 65536
DOC_MAX = 16384


def draw_queries(key, part):
    key = jax.random.fold_in(key, 1)
    base = jnp.clip(jax.random.normal(key, (SEQ, HEADS * HEAD), jnp.float32), -6.0, 6.0)
    return base.astype(jnp.bfloat16)


def draw_keys(key, part):
    key = jax.random.fold_in(key, 2)
    base = jnp.clip(jax.random.normal(key, (SEQ, HEAD), jnp.float32), -6.0, 6.0)
    return base.astype(jnp.bfloat16)


def block_scale(own_key, extent, split, least, top_value):
    def one(dim, blocks):
        steps = jax.random.uniform(jax.random.fold_in(jax.random.fold_in(own_key, 6), dim), (blocks,), jnp.float32, least / len(split), top_value / len(split))
        return jnp.repeat(jnp.exp(steps), extent[dim] // blocks).reshape((-1,) + (1,) * (len(extent) - dim - 1))

    factor_of = one(*split[0])
    for cut in split[1:]:
        factor_of = factor_of * one(*cut)
    return factor_of


def profile(amount, total, most, slope):
    portions = [(1 << 20) // math.isqrt(rank ** slope) + 1 for rank in range(2, amount + 1)]
    surplus, holding = total - most - (amount - 1), [1] * (amount - 1)
    while surplus > 0:
        movable = [i for i in range(amount - 1) if holding[i] < most]
        pool, left = sum([portions[i] for i in movable]), surplus
        for i in movable:
            extra = min(most - holding[i], max(1, left * portions[i] // pool), surplus)
            holding[i] = holding[i] + extra
            surplus = surplus - extra
    return np.array([most] + holding)


def uneven(stream_key, count, total, reach, skew):
    if count == 2:
        one = jax.random.randint(stream_key, (), max(1, total - reach), min(reach, total - 1) + 1)
        return jnp.stack([one, total - one])
    tallies = jnp.asarray(profile(count, total, reach, skew), jnp.int32)
    twos = (count - 1) // 2
    giver, taker = tallies[1:1 + 2 * twos:2], tallies[2:2 + 2 * twos:2]
    slack = jnp.minimum(giver - 1, reach - taker)
    passed = jax.random.randint(jax.random.fold_in(stream_key, 1), (twos,), 0, 1 << 20) % (slack + 1)
    tallies = tallies.at[1:1 + 2 * twos:2].set(giver - passed).at[2:2 + 2 * twos:2].set(taker + passed)
    return tallies[jax.random.permutation(jax.random.fold_in(stream_key, 2), count)]


def centred(stream_key, dims, scale, limit, shards=(), kind=jnp.bfloat16):
    entries = jax.random.normal(stream_key, dims, jnp.float32) * scale
    if len(shards) > 0:
        entries = block_scale(stream_key, dims, shards, -0.22, 0.18) * entries
    return jnp.clip(entries, min=-limit, max=limit).astype(kind)


def setup_inputs(seed: int = 0) -> dict:
    seeds = jax.random.split(jax.random.key(seed), 5)
    return {
        "queries": draw_queries(jax.random.fold_in(seeds[4], 71), 0),
        "keys": draw_keys(jax.random.fold_in(seeds[4], 71), 0),
        "values": centred(seeds[2], (SEQ, HEAD), 1.0, 6.0, ((0, 512),)),
        "lengths": uneven(seeds[3], DOCS, SEQ, DOC_MAX, 1).astype(jnp.int32),
    }


def doc_of(positions, ends):
    return jnp.sum((positions[:, None] >= ends[None, :]).astype(jnp.int32), axis=1).astype(jnp.int32)


def reference(queries, keys, values, lengths):
    block_rows = math.gcd(SEQ, 512)
    span = DOC_MAX + block_rows
    ends = jnp.cumsum(lengths).astype(jnp.int32)
    scale = HEAD ** -0.5
    pad_keys = jnp.concatenate([jnp.zeros((DOC_MAX, HEAD), keys.dtype), keys], axis=0)
    pad_values = jnp.concatenate([jnp.zeros((DOC_MAX, HEAD), values.dtype), values], axis=0)

    def one_block(block_index):
        start = (block_index * block_rows).astype(jnp.int32)
        query_block = lax.dynamic_slice(queries, (start, jnp.int32(0)), (block_rows, HEADS * HEAD))
        query_block = query_block.astype(jnp.float32).reshape(block_rows, HEADS, HEAD)
        key_block = lax.dynamic_slice(pad_keys, (start, jnp.int32(0)), (span, HEAD)).astype(jnp.float32)
        value_block = lax.dynamic_slice(pad_values, (start, jnp.int32(0)), (span, HEAD)).astype(jnp.float32)
        query_pos = start + jnp.arange(block_rows, dtype=jnp.int32)
        key_pos = start - DOC_MAX + jnp.arange(span, dtype=jnp.int32)
        allowed = (key_pos[None, :] <= query_pos[:, None]) & (key_pos[None, :] >= 0)
        allowed = allowed & (doc_of(key_pos, ends)[None, :] == doc_of(query_pos, ends)[:, None])
        scores = jnp.einsum('qhd,kd->hqk', query_block, key_block) * scale
        masked = jnp.where(allowed[None], scores, jnp.float32(-1e30))
        peak = jnp.max(masked, axis=-1)
        weights = jnp.where(allowed[None], jnp.exp(masked - peak[..., None]), jnp.float32(0.0))
        total = jnp.sum(weights, axis=-1)
        rounded = weights.astype(jnp.bfloat16).astype(jnp.float32)
        summed = jnp.einsum('hqk,kd->hqd', rounded, value_block) / total[..., None]
        return jnp.transpose(summed, (1, 0, 2)).reshape(block_rows, HEADS * HEAD).astype(jnp.bfloat16)

    blocks = lax.map(one_block, jnp.arange(SEQ // block_rows, dtype=jnp.int32))
    return blocks.reshape(SEQ, HEADS * HEAD)
```

```python
import functools
import math

import jax
import jax.numpy as jnp
from jax import lax
from jax.experimental import pallas as pl
from jax.experimental.pallas import tpu as pltpu
from jax.sharding import PartitionSpec as P

AXES = ("inner", "outer")
HEAD = 128
HEADS = 8
TOKENS = 128
ROWS = HEADS * TOKENS
SPAN = 16384
SCALE = HEAD**-0.5 * math.log2(math.e)
ROOM = 50.0
LARGEST_KEY = 6.0
HEADROOM = 100.0
LOWEST = -float(2**66)
MASKED = -1e30
STATS = 16


def coords(i):
    inner, outer = divmod(i, 32)
    return dict(zh=inner // 8, u=inner // 4 % 2, xp=inner // 2 % 2, c=inner % 2, y=outer // 8, w=outer // 2 % 4, zp=outer % 2)


def index(d):
    inner = d["zh"] * 8 + d["u"] * 4 + d["xp"] * 2 + d["c"]
    return inner * 32 + d["y"] * 8 + d["w"] * 2 + d["zp"]


def move(x, f):
    pairs = []
    for i in range(512):
        d = coords(i)
        to = f(**d)
        if to is not None:
            pairs.append((i, index({**d, **to})))
    return lax.ppermute(x, AXES, pairs)


def to_next_span(zh, u, xp, y, w, **_):
    span = 2 * zh + u + 1
    if span > 3:
        return None
    return dict(zh=span // 2, u=span % 2, xp=xp ^ (y & 1), w=3 - w if span == 2 else w)


def prep_kv_kernel(k_ref, v_ref, o_ref):
    o_ref[0] = k_ref[...]
    o_ref[1] = v_ref[...].T


def halves(x):
    high = x.astype(jnp.bfloat16).astype(jnp.float32)
    return high, (x - high).astype(jnp.bfloat16).astype(jnp.float32)


def stacked(row, *rows):
    out = jnp.zeros(row.shape, jnp.float32)
    for i, x in enumerate(rows):
        out = jnp.where(row == i, x, out)
    return out.astype(jnp.bfloat16)


def prep_q_kernel(q_ref, k_ref, o_ref):
    key_t = k_ref[...].T.astype(jnp.float32)
    row = lax.broadcasted_iota(jnp.int32, (STATS, TOKENS), 0)
    for h in range(HEADS):
        s = slice(h * HEAD, (h + 1) * HEAD)
        query_t = q_ref[:, s].T
        o_ref[:HEAD, s] = query_t
        query = query_t.astype(jnp.float32)
        shift = jnp.sum(query * key_t, axis=0, keepdims=True) * SCALE + ROOM
        high, low = halves(shift)
        highest = jnp.sum(jnp.abs(query), axis=0, keepdims=True) * (LARGEST_KEY * SCALE)
        unsafe = jnp.where(highest - shift > HEADROOM, 1.0, 0.0)
        o_ref[HEAD:, s] = stacked(row, high, low, unsafe)


def per_head(allowed, x, other):
    return jnp.concatenate(
        [jnp.where(allowed, x[:, h * TOKENS : (h + 1) * TOKENS], other) for h in range(HEADS)], axis=1
    )


def fold(pos, info, tiles, qi, q_at, qt_ref, at, row_ref, m_ref, l_ref, acc_ref):
    q_first, start_first, start_last, unsafe = (info[4 * qi + j] for j in range(4))
    for number, blocks in enumerate(tiles):

        def one(src, carry, number=number, blocks=blocks):
            places = [pos[(2 * number + src) * len(blocks) + j] for j in range(len(blocks))]
            low = functools.reduce(jnp.minimum, places)
            high = functools.reduce(jnp.maximum, places) + (TOKENS - 1)
            active = (high >= start_first) & (low <= q_first + (TOKENS - 1))
            whole = (high <= q_first) & (low >= start_last)
            safe = unsafe == 0

            def visit(masked, online):
                key = jnp.concatenate([ref[j, src, 0] for ref, j in blocks], axis=0)
                value_t = jnp.concatenate([ref[j, src, 1] for ref, j in blocks], axis=1)
                if masked:
                    iota = lax.broadcasted_iota(jnp.int32, (TOKENS, TOKENS), 0)
                    key_pos = jnp.concatenate([iota + p for p in places], axis=0)
                    allowed = (key_pos <= row_ref[q_at, 0:1]) & (key_pos >= row_ref[q_at, 1:2])
                scores = lax.dot(key, qt_ref[q_at, :HEAD], preferred_element_type=jnp.float32)
                if not online:
                    weights = jnp.exp2(scores * SCALE - m_ref[at])
                    if masked:
                        weights = per_head(allowed, weights, 0.0)
                    l_ref[at] += jnp.sum(weights, axis=0, keepdims=True)
                    acc_ref[at] += lax.dot(
                        value_t, weights.astype(jnp.bfloat16), preferred_element_type=jnp.float32
                    )
                    return
                scores = per_head(allowed, scores, MASKED)
                old = m_ref[at]
                new = jnp.maximum(old, jnp.max(scores, axis=0, keepdims=True) * SCALE)
                weights = jnp.exp2(scores * SCALE - new)
                factor = jnp.exp2(old - new)
                m_ref[at] = new
                l_ref[at] = l_ref[at] * factor + jnp.sum(weights, axis=0, keepdims=True)
                acc_ref[at] = acc_ref[at] * factor + lax.dot(
                    value_t, weights.astype(jnp.bfloat16), preferred_element_type=jnp.float32
                )

            @pl.when(active & whole & safe)
            def _():
                visit(False, False)

            @pl.when(active & jnp.logical_not(whole) & safe)
            def _():
                visit(True, False)

            @pl.when(active & jnp.logical_not(safe))
            def _():
                visit(True, True)

            return carry

        lax.fori_loop(0, 2, one, 0)


def tiles_of(shape, refs):
    return [[(refs[a], j) for a, j in blocks] for blocks in shape]


def part_kernel(shape, n, pos, info, *refs):
    tiles, (qt_ref, row_ref, m_ref, l_ref, acc_ref) = tiles_of(shape, refs), refs[n:]
    l_ref[...] = jnp.zeros_like(l_ref)
    acc_ref[...] = jnp.zeros_like(acc_ref)

    def one(qi, carry):
        rows = qt_ref[qi, HEAD:].astype(jnp.float32)
        m_ref[qi] = jnp.where(info[4 * qi + 3] == 0, rows[0:1] + rows[1:2], LOWEST)
        fold(pos, info, tiles, qi, qi, qt_ref, qi, row_ref, m_ref, l_ref, acc_ref)
        return carry

    lax.fori_loop(0, 4, one, 0)


def last_kernel(shape, n, states, qi, pos, info, *refs):
    tiles, rest = tiles_of(shape, refs), refs[n:]
    qt_ref, row_ref, *parts = rest[: 2 + 3 * states]
    out_ref, m_ref, l_ref, acc_ref = rest[2 + 3 * states :]
    peaks = [parts[3 * i][0] for i in range(states)]
    top = functools.reduce(jnp.maximum, peaks)
    factors = [jnp.exp2(p - top) for p in peaks]
    m_ref[0] = top
    l_ref[0] = sum(parts[3 * i + 1][0] * factors[i] for i in range(states))
    acc_ref[0] = sum(parts[3 * i + 2][0] * factors[i] for i in range(states))
    fold(pos, info, tiles, qi, 0, qt_ref, 0, row_ref, m_ref, l_ref, acc_ref)
    high, low = halves(m_ref[0])
    factor = jnp.exp2(m_ref[0] - (high + low))
    out_ref[:HEAD] = (acc_ref[0] * factor).astype(jnp.bfloat16)
    row = lax.broadcasted_iota(jnp.int32, (STATS, ROWS), 0)
    out_ref[HEAD:] = stacked(row, high, low, *halves(l_ref[0] * factor))


def combine_kernel(a_ref, b_ref, c_ref, d_ref, out_ref):
    refs = (a_ref, b_ref, c_ref, d_ref)
    stats = [r[HEAD:].astype(jnp.float32) for r in refs]
    peaks = [s[0:1] + s[1:2] for s in stats]
    top = functools.reduce(jnp.maximum, peaks)
    factors = [jnp.exp2(p - top) for p in peaks]
    total = sum(f * (s[2:3] + s[3:4]) for f, s in zip(factors, stats))
    inverse = [f / total for f in factors]
    for h in range(HEADS):
        s = slice(h * TOKENS, (h + 1) * TOKENS)
        summed = sum(i[:, s] * r[:HEAD, s].astype(jnp.float32) for i, r in zip(inverse, refs))
        out_ref[:, s] = summed.T.astype(jnp.bfloat16)


VMEM = pl.BlockSpec(memory_space=pltpu.VMEM)
SMEM = pl.BlockSpec(memory_space=pltpu.SMEM)


def params(mib=24):
    return pltpu.CompilerParams(vmem_limit_bytes=mib * 2**20)


def cost(tiles):
    return pl.CostEstimate(flops=tiles * 4 * 512 * ROWS * HEAD, bytes_accessed=tiles * 2**18, transcendentals=tiles * 512 * ROWS)


def state_shapes():
    return [
        jax.ShapeDtypeStruct((4, 1, ROWS), jnp.float32),
        jax.ShapeDtypeStruct((4, 1, ROWS), jnp.float32),
        jax.ShapeDtypeStruct((4, HEAD, ROWS), jnp.float32),
    ]


def part_call(shape, pos, info, arrays, qt, rows, name):
    n = len(arrays)
    return pl.pallas_call(
        functools.partial(part_kernel, shape, n),
        out_shape=state_shapes(),
        in_specs=[SMEM, SMEM] + [VMEM] * (n + 2),
        out_specs=[VMEM] * 3,
        compiler_params=params(),
        cost_estimate=cost(8),
        name=name,
    )(pos, info, *arrays, qt, rows)


def last_call(qi, shape, pos, info, arrays, qt, rows, states):
    n = len(arrays)

    def whole(dims):
        return pl.BlockSpec(dims, lambda i: (0,) * len(dims))

    def part(*dims):
        return pl.BlockSpec((1, *dims), lambda i: (qi, 0, 0))

    return pl.pallas_call(
        functools.partial(last_kernel, shape, n, len(states), qi),
        grid=(1,),
        out_shape=jax.ShapeDtypeStruct((HEAD + STATS, ROWS), jnp.bfloat16),
        in_specs=[SMEM, SMEM]
        + [whole(a.shape) for a in arrays]
        + [part(HEAD + STATS, ROWS), part(8, TOKENS)]
        + [part(1, ROWS), part(1, ROWS), part(HEAD, ROWS)] * len(states),
        out_specs=whole((HEAD + STATS, ROWS)),
        scratch_shapes=[
            pltpu.VMEM((1, 1, ROWS), jnp.float32),
            pltpu.VMEM((1, 1, ROWS), jnp.float32),
            pltpu.VMEM((1, HEAD, ROWS), jnp.float32),
        ],
        compiler_params=params(),
        cost_estimate=cost(2),
        name="last",
    )(pos, info, *arrays, qt, rows, *[x for state in states for x in state])


def shards(queries, keys, values, lengths):
    inner = lax.axis_index("inner")
    outer = lax.axis_index("outer")
    span, xp, c = inner // 4, inner // 2 % 2, inner % 2
    y, w, zp = outer // 8, outer // 2 % 4, outer % 2

    def places(cc, yy):
        out = []
        for src in range(2):
            for j in range(4):
                ww = w ^ jnp.where(cc == 0, (0, 2, 1, 3)[j], j)
                if src == 1:
                    ww = jnp.where(span == 2, 3 - ww, ww)
                out.append(
                    SPAN * (span - src) + 8192 * (xp ^ (yy & 1)) + 4096 * cc + 1024 * yy + 256 * ww + 128 * zp
                )
        return out

    def near(cc):
        return jnp.where(cc == 0, y ^ 1, 3 - y)

    def table(*lists):
        return jnp.stack([p for part in lists for p in part]).astype(jnp.int32)

    o = 1 - c
    pos_own = table(places(c, y), places(o, y))
    pos_near = table(places(c, near(c)), places(o, near(o)))
    pos_far = table(places(c, near(o)), places(c, (y + 2) % 4))
    pos_far_o = table(places(o, near(c)), places(o, (y + 2) % 4))

    ends = jnp.cumsum(lengths).astype(jnp.int32)
    q_first = jnp.stack(
        [
            SPAN * span
            + 8192 * (xp ^ jnp.where(c == 0, s // 2, s % 2))
            + 4096 * c
            + 1024 * y
            + 256 * w
            + 128 * (zp ^ jnp.where(c == 0, s % 2, s // 2))
            for s in range(4)
        ]
    ).astype(jnp.int32)
    q_pos = q_first[:, None] + jnp.arange(TOKENS, dtype=jnp.int32)[None]
    q_start = jnp.max(jnp.where(ends[None, None, :] <= q_pos[:, :, None], ends[None, None, :], 0), axis=2)
    rows = jnp.concatenate(
        [q_pos[:, None], q_start[:, None], jnp.zeros((4, 6, TOKENS), jnp.int32)], axis=1
    )

    raw = pl.pallas_call(
        prep_kv_kernel,
        out_shape=jax.ShapeDtypeStruct((2, TOKENS, HEAD), jnp.bfloat16),
        in_specs=[VMEM] * 2,
        out_specs=VMEM,
        name="prep_kv",
    )(keys, values)
    qt = pl.pallas_call(
        prep_q_kernel,
        out_shape=jax.ShapeDtypeStruct((HEAD + STATS, ROWS), jnp.bfloat16),
        in_specs=[VMEM] * 2,
        out_specs=VMEM,
        name="prep_q",
    )(queries, keys)

    with jax.named_scope("keys_x"):
        before = move(raw, to_next_span)
        mine = move(raw, lambda xp, y, **_: dict(xp=xp ^ (y & 1)))
    def to_slot(s):
        def f(c, xp, zp, **_):
            x, z = (s // 2, s % 2) if c == 0 else (s % 2, s // 2)
            return dict(xp=xp ^ x, zp=zp ^ z)

        return f

    with jax.named_scope("queries_1"):
        q1 = move(qt, to_slot(1))
    with jax.named_scope("keys_z1"):
        held = jnp.stack([mine, before])[None]
        got = move(held, lambda w, c, **_: dict(w=w ^ (1 if c else 2)))
    with jax.named_scope("queries_2"):
        q2 = jnp.stack([qt, q1])
        q4 = jnp.concatenate([q2, move(q2, to_slot(2))], axis=0)
        unsafe = jnp.max(q4[:, HEAD + 2].astype(jnp.float32), axis=1)
        unsafe = (unsafe > 0.5).astype(jnp.int32)
        info = jnp.stack([q_first, q_start[:, 0], q_start[:, -1], unsafe], axis=1).reshape(-1)
    with jax.named_scope("keys_z2"):
        held = jnp.concatenate([held, got], axis=0)
        got = move(held, lambda w, c, **_: dict(w=w ^ (2 if c else 1)))
        held = jnp.concatenate([held, got], axis=0)

    def swap(x):
        return move(x, lambda c, **_: dict(c=1 - c))

    two_arrays = tuple(tuple((a, j) for j in range(4)) for a in range(2))
    one_array = tuple(tuple((0, 4 * a + j) for j in range(4)) for a in range(2))
    with jax.named_scope("keys_y1"):
        got = move(held, lambda y, c, **_: dict(y=3 - y if c else y ^ 1))
    with jax.named_scope("keys_c0"):
        held_o = swap(held)
    with jax.named_scope("keys_y2"):
        both = jnp.concatenate([held, got], axis=0)
        far = move(both, lambda y, c, **_: dict(y=y ^ 1 if c else 3 - y))
    with jax.named_scope("keys_c1"):
        got_o = swap(got)
    states = [
        part_call(two_arrays, pos_own, info, [held, held_o], q4, rows, "own"),
        part_call(two_arrays, pos_near, info, [got, got_o], q4, rows, "near"),
    ]
    far, states = lax.optimization_barrier((far, states))
    with jax.named_scope("keys_c2"):
        far_o = swap(far)
    states.append(part_call(one_array, pos_far, info, [far], q4, rows, "far"))
    parts = []
    for s in (3, 2, 1, 0):
        part = last_call(s, one_array, pos_far_o, info, [far_o], q4, rows, states)
        if s:
            with jax.named_scope("sums"):
                part = move(part, to_slot(s))
        parts.append(part)
    return pl.pallas_call(
        combine_kernel,
        out_shape=jax.ShapeDtypeStruct((TOKENS, ROWS), jnp.bfloat16),
        in_specs=[VMEM] * 4,
        out_specs=VMEM,
        compiler_params=params(),
        name="combine",
    )(*parts)


def solution(mesh):
    spec = P(AXES, None)
    return jax.shard_map(shards, mesh=mesh, in_specs=(spec, spec, spec, P()), out_specs=spec, check_vma=False)
```

```python
import functools
import math

import jax
import jax.numpy as jnp
from jax import lax
from jax.experimental import pallas as pl
from jax.experimental.pallas import tpu as pltpu
from jax.sharding import PartitionSpec as P

AXES = ("inner", "outer")
HEAD = 128
HEADS = 8
TOKENS = 128
DOCS = 16
ROWS = HEADS * TOKENS
SPAN = 16384
SCALE = HEAD**-0.5 * math.log2(math.e)
ROOM = 50.0
LARGEST_KEY = 6.0
HEADROOM = 100.0
LOWEST = -float(2**66)
MASKED = -1e30
STATS = 16


def coords(i):
    inner, outer = divmod(i, 32)
    return dict(zh=inner // 8, u=inner // 4 % 2, xp=inner // 2 % 2, c=inner % 2, y=outer // 8, w=outer // 2 % 4, zp=outer % 2)


def index(d):
    inner = d["zh"] * 8 + d["u"] * 4 + d["xp"] * 2 + d["c"]
    return inner * 32 + d["y"] * 8 + d["w"] * 2 + d["zp"]


def move(x, f):
    pairs = []
    for i in range(512):
        d = coords(i)
        to = f(**d)
        if to is not None:
            pairs.append((i, index({**d, **to})))
    return lax.ppermute(x, AXES, pairs)


def to_next_span(zh, u, xp, y, w, **_):
    span = 2 * zh + u + 1
    if span > 3:
        return None
    return dict(zh=span // 2, u=span % 2, xp=xp ^ (y & 1), w=3 - w if span == 2 else w)


def halves(x):
    high = x.astype(jnp.bfloat16).astype(jnp.float32)
    return high, (x - high).astype(jnp.bfloat16).astype(jnp.float32)


def stacked(row, *rows):
    out = jnp.zeros(row.shape, jnp.float32)
    for i, x in enumerate(rows):
        out = jnp.where(row == i, x, out)
    return out.astype(jnp.bfloat16)


def prep_kernel(q_ref, k_ref, o_ref):
    key_t = k_ref[...].T.astype(jnp.float32)
    row = lax.broadcasted_iota(jnp.int32, (STATS, TOKENS), 0)
    for h in range(HEADS):
        s = slice(h * HEAD, (h + 1) * HEAD)
        query_t = q_ref[:, s].T
        o_ref[:HEAD, s] = query_t
        query = query_t.astype(jnp.float32)
        shift = jnp.sum(query * key_t, axis=0, keepdims=True) * SCALE + ROOM
        high, low = halves(shift)
        highest = jnp.sum(jnp.abs(query), axis=0, keepdims=True) * (LARGEST_KEY * SCALE)
        unsafe = jnp.where(highest - shift > HEADROOM, 1.0, 0.0)
        o_ref[HEAD:, s] = stacked(row, high, low, unsafe)


def pair_kernel(a_ref, b_ref, out_ref):
    for i, ref in enumerate((a_ref, b_ref)):
        out_ref[0, i, 0] = ref[0]
        out_ref[0, i, 1] = ref[1].T


def join_kernel(*refs):
    *in_refs, out_ref = refs
    at = 0
    for ref in in_refs:
        out_ref[at : at + ref.shape[0]] = ref[...]
        at += ref.shape[0]


def near(y, cc):
    return jnp.where(cc == 0, y ^ 1, 3 - y)


def place(cd, flip, kind, src, slot):
    span, xp, c, y, w, zp = (cd[i] for i in range(6))
    cc = c ^ flip
    yy = {"own": y, "one": near(y, cc), "two": near(y, 1 - cc), "far": (y + 2) & 3}[kind]
    ww = w ^ jnp.where(cc == 0, (0, 2, 1, 3)[slot], slot)
    ww = jnp.where((src == 1) & (span == 2), 3 - ww, ww)
    return SPAN * (span - src) + 8192 * (xp ^ (yy & 1)) + 4096 * cc + 1024 * yy + 256 * ww + 128 * zp


def first_of(cd, qi):
    span, xp, c, y, w, zp = (cd[i] for i in range(6))
    return SPAN * span + 8192 * (xp ^ (qi >> 1)) + 4096 * c + 1024 * y + 256 * w + 128 * (zp ^ (qi & 1))


def start_of(lengths, positions):
    end, start = jnp.int32(0), jnp.zeros_like(positions)
    for d in range(DOCS):
        end = end + lengths[d]
        start = jnp.where(end <= positions, end, start)
    return start


def per_head(allowed, x, other):
    return jnp.concatenate(
        [jnp.where(allowed, x[:, h * TOKENS : (h + 1) * TOKENS], other) for h in range(HEADS)], axis=1
    )


def fold(cd, lengths, info, tiles, qi, qt_ref, at, m_ref, l_ref, acc_ref):
    q_first, start_first, start_last, unsafe = (info[4 * qi + j] for j in range(4))
    safe = unsafe == 0

    def visit(src, blocks, places, masked, online):
        key = jnp.concatenate([ref[j, src, 0] for ref, j in blocks], axis=0)
        value_t = jnp.concatenate([ref[j, src, 1] for ref, j in blocks], axis=1)
        if masked:
            iota = lax.broadcasted_iota(jnp.int32, (TOKENS, TOKENS), 0)
            key_pos = jnp.concatenate([iota + p for p in places], axis=0)
            query_pos = q_first + lax.broadcasted_iota(jnp.int32, (1, TOKENS), 1)
            allowed = (key_pos <= query_pos) & (key_pos >= start_of(lengths, query_pos))
        scores = lax.dot(key, qt_ref[qi, :HEAD], preferred_element_type=jnp.float32)
        if not online:
            weights = jnp.exp2(scores * SCALE - m_ref[at])
            if masked:
                weights = per_head(allowed, weights, 0.0)
            l_ref[at] += jnp.sum(weights, axis=0, keepdims=True)
            acc_ref[at] += lax.dot(value_t, weights.astype(jnp.bfloat16), preferred_element_type=jnp.float32)
            return
        scores = per_head(allowed, scores, MASKED)
        old = m_ref[at]
        new = jnp.maximum(old, jnp.max(scores, axis=0, keepdims=True) * SCALE)
        weights = jnp.exp2(scores * SCALE - new)
        factor = jnp.exp2(old - new)
        m_ref[at] = new
        l_ref[at] = l_ref[at] * factor + jnp.sum(weights, axis=0, keepdims=True)
        acc_ref[at] = acc_ref[at] * factor + lax.dot(
            value_t, weights.astype(jnp.bfloat16), preferred_element_type=jnp.float32
        )

    def one(src, carry):
        found = []
        for flip, kind, blocks in tiles:
            places = [place(cd, flip, kind, src, j) for j in range(4)]
            low = functools.reduce(jnp.minimum, places)
            high = functools.reduce(jnp.maximum, places) + (TOKENS - 1)
            active = (high >= start_first) & (low <= q_first + (TOKENS - 1))
            whole = active & (high <= q_first) & (low >= start_last) & safe
            found.append((blocks, places, active, whole))
        together = False
        if len(found) == 2:
            together = found[0][3] & found[1][3]

            @pl.when(together)
            def _():
                visit(src, found[0][0] + found[1][0], None, False, False)

        for blocks, places, active, whole in found:

            @pl.when(whole & jnp.logical_not(together))
            def _(blocks=blocks, places=places):
                visit(src, blocks, places, False, False)

            @pl.when(active & jnp.logical_not(whole) & safe)
            def _(blocks=blocks, places=places):
                visit(src, blocks, places, True, False)

            @pl.when(active & jnp.logical_not(safe))
            def _(blocks=blocks, places=places):
                visit(src, blocks, places, True, True)

        return carry

    lax.fori_loop(0, 2, one, 0)


def tiles_of(kinds, refs):
    out = []
    for (flip, names), ref in zip(kinds, refs):
        out += [(flip, name, [(ref, 4 * i + j) for j in range(4)]) for i, name in enumerate(names)]
    return out


def own_kernel(kinds, n, cd, lengths, *refs):
    tiles, rest = tiles_of(kinds, refs), refs[n:]
    a_ref, b_ref, c_ref, info, qt_ref, m_ref, l_ref, acc_ref = rest
    qt_ref[0] = a_ref[...]
    qt_ref[1] = b_ref[...]
    qt_ref[2:] = c_ref[...]

    def one(qi, carry):
        rows = qt_ref[qi, HEAD:].astype(jnp.float32)
        unsafe = (jnp.max(rows[2:3]) > 0.5).astype(jnp.int32)
        q_first = first_of(cd, qi)
        info[4 * qi] = q_first
        info[4 * qi + 1] = start_of(lengths, q_first)
        info[4 * qi + 2] = start_of(lengths, q_first + (TOKENS - 1))
        info[4 * qi + 3] = unsafe
        m_ref[qi] = jnp.where(unsafe == 0, rows[0:1] + rows[1:2], LOWEST)
        l_ref[qi] = jnp.zeros_like(l_ref[qi])
        acc_ref[qi] = jnp.zeros_like(acc_ref[qi])
        fold(cd, lengths, info, tiles, qi, qt_ref, qi, m_ref, l_ref, acc_ref)
        return carry

    lax.fori_loop(0, 4, one, 0)


def part_kernel(kinds, n, cd, lengths, info, *refs):
    tiles, (qt_ref, *state, m_ref, l_ref, acc_ref) = tiles_of(kinds, refs), refs[n:]

    def one(qi, carry):
        m_ref[qi], l_ref[qi], acc_ref[qi] = (r[qi] for r in state)
        fold(cd, lengths, info, tiles, qi, qt_ref, qi, m_ref, l_ref, acc_ref)
        return carry

    lax.fori_loop(0, 4, one, 0)


def last_kernel(kinds, n, qis, cd, lengths, info, *refs):
    tiles, (qt_ref, *state) = tiles_of(kinds, refs), refs[n : n + 4]
    *out_refs, m_ref, l_ref, acc_ref = refs[n + 4 :]
    for qi, out_ref in zip(qis, out_refs):
        m_ref[0], l_ref[0], acc_ref[0] = (r[qi] for r in state)
        fold(cd, lengths, info, tiles, qi, qt_ref, 0, m_ref, l_ref, acc_ref)
        high, low = halves(m_ref[0])
        factor = jnp.exp2(m_ref[0] - (high + low))
        out_ref[:HEAD] = (acc_ref[0] * factor).astype(jnp.bfloat16)
        row = lax.broadcasted_iota(jnp.int32, (STATS, ROWS), 0)
        out_ref[HEAD:] = stacked(row, high, low, *halves(l_ref[0] * factor))


def unpacked(ref):
    stats = ref[HEAD:].astype(jnp.float32)
    return stats[0:1] + stats[1:2], stats[2:3] + stats[3:4], ref[:HEAD]


def final_kernel(kinds, n, cd, lengths, info, *refs):
    tiles, (qt_ref, packed_ref, *state) = tiles_of(kinds, refs), refs[n : n + 5]
    m_ref, l_ref, acc_ref = refs[n + 5 :]
    m_ref[0], l_ref[0], acc_ref[0] = (r[0] for r in state)
    fold(cd, lengths, info, tiles, 0, qt_ref, 0, m_ref, l_ref, acc_ref)
    m_a, l_a, acc_a = unpacked(packed_ref)
    m_b = m_ref[0]
    top = jnp.maximum(m_a, m_b)
    f_a, f_b = jnp.exp2(m_a - top), jnp.exp2(m_b - top)
    m_ref[0] = top
    l_ref[0] = l_a * f_a + l_ref[0] * f_b
    acc_ref[0] = acc_a.astype(jnp.float32) * f_a + acc_ref[0] * f_b


def combine_kernel(a_ref, b_ref, m_ref, l_ref, acc_ref, out_ref):
    states = [unpacked(a_ref), unpacked(b_ref), (m_ref[0], l_ref[0], acc_ref[0])]
    top = functools.reduce(jnp.maximum, [m for m, _, _ in states])
    factors = [jnp.exp2(m - top) for m, _, _ in states]
    total = sum(f * l for f, (_, l, _) in zip(factors, states))
    inverse = [f / total for f in factors]
    for h in range(HEADS):
        s = slice(h * TOKENS, (h + 1) * TOKENS)
        summed = sum(i[:, s] * acc[:, s].astype(jnp.float32) for i, (_, _, acc) in zip(inverse, states))
        out_ref[:, s] = summed.T.astype(jnp.bfloat16)


VMEM = pl.BlockSpec(memory_space=pltpu.VMEM)
SMEM = pl.BlockSpec(memory_space=pltpu.SMEM)
LONG = 2**13
STATE = [
    jax.ShapeDtypeStruct((4, 1, ROWS), jnp.float32),
    jax.ShapeDtypeStruct((4, 1, ROWS), jnp.float32),
    jax.ShapeDtypeStruct((4, HEAD, ROWS), jnp.float32),
]
PACKED = jax.ShapeDtypeStruct((HEAD + STATS, ROWS), jnp.bfloat16)
SCRATCH = [
    pltpu.VMEM((1, 1, ROWS), jnp.float32),
    pltpu.VMEM((1, 1, ROWS), jnp.float32),
    pltpu.VMEM((1, HEAD, ROWS), jnp.float32),
]


def call(kernel, name, out_shape, scalars, arrays, out_specs, cost=1, scratch=()):
    return pl.pallas_call(
        kernel,
        out_shape=out_shape,
        in_specs=[SMEM] * len(scalars) + [VMEM] * len(arrays),
        out_specs=out_specs,
        scratch_shapes=list(scratch),
        compiler_params=pltpu.CompilerParams(vmem_limit_bytes=16 * 2**20),
        cost_estimate=pl.CostEstimate(
            flops=cost * 2**20, bytes_accessed=cost * 2**10, transcendentals=cost * 2**10
        ),
        name=name,
    )(*scalars, *arrays)


def join(*arrays):
    shape = (sum(a.shape[0] for a in arrays), *arrays[0].shape[1:])
    return call(join_kernel, "join", jax.ShapeDtypeStruct(shape, jnp.bfloat16), (), arrays, VMEM)


def shards(queries, keys, values, lengths):
    table = [[2 * d["zh"] + d["u"], d["xp"], d["c"], d["y"], d["w"], d["zp"], 0, 0] for d in map(coords, range(512))]
    me = lax.axis_index("inner") * 32 + lax.axis_index("outer")
    cd = lax.dynamic_slice(jnp.asarray(table, jnp.int32), (me, 0), (1, 8)).reshape(8)
    scalars = (cd, lengths)

    def to_slot(s):
        return lambda xp, zp, **_: dict(xp=xp ^ (s // 2), zp=zp ^ (s % 2))

    def swap(x):
        return move(x, lambda c, **_: dict(c=1 - c))

    raw = jnp.stack([keys, values])
    qt = pl.pallas_call(prep_kernel, out_shape=PACKED, in_specs=[VMEM] * 2, out_specs=VMEM, name="prep")(
        queries, keys
    )
    with jax.named_scope("queries_z"):
        qz = move(qt, to_slot(1))

    with jax.named_scope("keys_x"):
        before = move(raw, to_next_span)
        mine = move(raw, lambda xp, y, **_: dict(xp=xp ^ (y & 1)))
    with jax.named_scope("keys_z1"):
        shape = jax.ShapeDtypeStruct((1, 2, 2, TOKENS, HEAD), jnp.bfloat16)
        held = call(pair_kernel, "pair", shape, (), [mine, before], VMEM, LONG)
        got = move(held, lambda w, c, **_: dict(w=w ^ (1 if c else 2)))
    with jax.named_scope("queries_x"):
        qx = move(jnp.stack([qt, qz]), to_slot(2))
    with jax.named_scope("keys_z2"):
        held = join(held, got)
        got = move(held, lambda w, c, **_: dict(w=w ^ (2 if c else 1)))
        held = join(held, got)
    with jax.named_scope("keys_y1"):
        one = move(held, lambda y, c, **_: dict(y=3 - y if c else y ^ 1))

    info, q4, *state = call(
        functools.partial(own_kernel, [(0, ["own"])], 1),
        "own",
        [jax.ShapeDtypeStruct((16,), jnp.int32), jax.ShapeDtypeStruct((4, *PACKED.shape), jnp.bfloat16)] + STATE,
        scalars,
        [held, qt, qz, qx],
        [SMEM] + [VMEM] * 4,
    )
    scalars = (cd, lengths, info)

    def part(name, kinds, arrays, state):
        kernel = functools.partial(part_kernel, kinds, len(arrays))
        return call(kernel, name, STATE, scalars, [*arrays, q4, *state], [VMEM] * 3)

    one, state = lax.optimization_barrier((one, state))
    with jax.named_scope("keys_y2"):
        both = join(held, one)
        far = move(both, lambda y, c, **_: dict(y=y ^ 1 if c else 3 - y))
    with jax.named_scope("keys_c1"):
        held_o = swap(held)
        one_o = swap(one)
    state = part("one", [(0, ["one"])], [one], state)
    state = part("other", [(1, ["own"]), (1, ["one"])], [held_o, one_o], state)
    far, state = lax.optimization_barrier((far, state))
    with jax.named_scope("keys_c2"):
        far_o = swap(far)
    state = part("far", [(0, ["two", "far"])], [far], state)
    kinds = [(1, ["two", "far"])]
    sent = {}
    for qis in ((3,), (2, 1)):
        kernel = functools.partial(last_kernel, kinds, 1, qis)
        packed = call(
            kernel, "last", [PACKED] * len(qis), scalars, [far_o, q4, *state], [VMEM] * len(qis), 1, SCRATCH
        )
        packed, state = lax.optimization_barrier((packed, state))
        sent.update(zip(qis, packed))
    with jax.named_scope("sums"):
        got = {s: move(sent[s], to_slot(s)) for s in (3, 2, 1)}
    shape = [jax.ShapeDtypeStruct((1, *x.shape[1:]), x.dtype) for x in STATE]
    kernel = functools.partial(final_kernel, kinds, 1)
    state = call(kernel, "final", shape, scalars, [far_o, q4, got[3], *state], [VMEM] * 3, LONG)
    out_shape = jax.ShapeDtypeStruct((TOKENS, ROWS), jnp.bfloat16)
    return call(combine_kernel, "combine", out_shape, (), [got[2], got[1], *state], VMEM)


def solution(mesh):
    spec = P(AXES, None)
    return jax.shard_map(shards, mesh=mesh, in_specs=(spec, spec, spec, P()), out_specs=spec, check_vma=False)
```

```python
import functools
import math

import jax
import jax.numpy as jnp
from jax import lax
from jax.experimental import pallas as pl
from jax.experimental.pallas import tpu as pltpu
from jax.sharding import PartitionSpec as P

AXES = ("inner", "outer")
HEAD = 128
HEADS = 8
TOKENS = 128
DOCS = 16
ROWS = HEADS * TOKENS
SPAN = 16384
SCALE = HEAD**-0.5 * math.log2(math.e)
ROOM = 50.0
LARGEST_KEY = 6.0
HEADROOM = 100.0
LOWEST = -float(2**66)
MASKED = -1e30
STATS = 16


def coords(i):
    inner, outer = divmod(i, 32)
    return dict(zh=inner // 8, u=inner // 4 % 2, xp=inner // 2 % 2, c=inner % 2, y=outer // 8, w=outer // 2 % 4, zp=outer % 2)


def index(d):
    inner = d["zh"] * 8 + d["u"] * 4 + d["xp"] * 2 + d["c"]
    return inner * 32 + d["y"] * 8 + d["w"] * 2 + d["zp"]


def move(x, f):
    pairs = []
    for i in range(512):
        d = coords(i)
        to = f(**d)
        if to is not None:
            pairs.append((i, index({**d, **to})))
    return lax.ppermute(x, AXES, pairs)


def to_next_span(zh, u, xp, y, w, **_):
    span = 2 * zh + u + 1
    if span > 3:
        return None
    return dict(zh=span // 2, u=span % 2, xp=xp ^ (y & 1), w=3 - w if span == 2 else w)


def halves(x):
    high = x.astype(jnp.bfloat16).astype(jnp.float32)
    return high, (x - high).astype(jnp.bfloat16).astype(jnp.float32)


def stacked(row, *rows):
    out = jnp.zeros(row.shape, jnp.float32)
    for i, x in enumerate(rows):
        out = jnp.where(row == i, x, out)
    return out.astype(jnp.bfloat16)


def prep_kernel(q_ref, k_ref, o_ref):
    key_t = k_ref[...].T.astype(jnp.float32)
    row = lax.broadcasted_iota(jnp.int32, (STATS, TOKENS), 0)
    for h in range(HEADS):
        s = slice(h * HEAD, (h + 1) * HEAD)
        query_t = q_ref[:, s].T
        o_ref[:HEAD, s] = query_t
        query = query_t.astype(jnp.float32)
        shift = jnp.sum(query * key_t, axis=0, keepdims=True) * SCALE + ROOM
        high, low = halves(shift)
        highest = jnp.sum(jnp.abs(query), axis=0, keepdims=True) * (LARGEST_KEY * SCALE)
        unsafe = jnp.where(highest - shift > HEADROOM, 1.0, 0.0)
        o_ref[HEAD:, s] = stacked(row, high, low, unsafe)


def pair_kernel(a_ref, b_ref, out_ref):
    for i, ref in enumerate((a_ref, b_ref)):
        out_ref[0, i, 0] = ref[0]
        out_ref[0, i, 1] = ref[1].T


def join_kernel(*refs):
    *in_refs, out_ref = refs
    at = 0
    for ref in in_refs:
        out_ref[at : at + ref.shape[0]] = ref[...]
        at += ref.shape[0]


def near(y, cc):
    return jnp.where(cc == 0, y ^ 1, 3 - y)


def place_of(cd):
    me = cd[0]
    return me >> 7, (me >> 6) & 1, (me >> 5) & 1, (me >> 3) & 3, (me >> 1) & 3, me & 1


def place(cd, flip, kind, src, slot):
    span, xp, c, y, w, zp = place_of(cd)
    cc = c ^ flip
    yy = {"own": y, "one": near(y, cc), "two": near(y, 1 - cc), "far": (y + 2) & 3}[kind]
    ww = w ^ jnp.where(cc == 0, (0, 2, 1, 3)[slot], slot)
    ww = jnp.where((src == 1) & (span == 2), 3 - ww, ww)
    return SPAN * (span - src) + 8192 * (xp ^ (yy & 1)) + 4096 * cc + 1024 * yy + 256 * ww + 128 * zp


def first_of(cd, qi):
    span, xp, c, y, w, zp = place_of(cd)
    return SPAN * span + 8192 * (xp ^ (qi >> 1)) + 4096 * c + 1024 * y + 256 * w + 128 * (zp ^ (qi & 1))


def start_of(lengths, positions):
    end, start = jnp.int32(0), jnp.zeros_like(positions)
    for d in range(DOCS):
        end = end + lengths[d]
        start = jnp.where(end <= positions, end, start)
    return start


def per_head(allowed, x, other):
    return jnp.concatenate(
        [jnp.where(allowed, x[:, h * TOKENS : (h + 1) * TOKENS], other) for h in range(HEADS)], axis=1
    )


def fold(cd, lengths, info, tiles, qi, qt_ref, at, m_ref, l_ref, acc_ref):
    q_first, start_first, start_last, unsafe = (info[4 * qi + j] for j in range(4))
    safe = unsafe == 0

    def visit(src, blocks, places, masked, online):
        key = jnp.concatenate([ref[j, src, 0] for ref, j in blocks], axis=0)
        value_t = jnp.concatenate([ref[j, src, 1] for ref, j in blocks], axis=1)
        if masked:
            iota = lax.broadcasted_iota(jnp.int32, (TOKENS, TOKENS), 0)
            key_pos = jnp.concatenate([iota + p for p in places], axis=0)
            query_pos = q_first + lax.broadcasted_iota(jnp.int32, (1, TOKENS), 1)
            allowed = (key_pos <= query_pos) & (key_pos >= start_of(lengths, query_pos))
        scores = lax.dot(key, qt_ref[qi, :HEAD], preferred_element_type=jnp.float32)
        if not online:
            weights = jnp.exp2(scores * SCALE - m_ref[at])
            if masked:
                weights = per_head(allowed, weights, 0.0)
            row = lax.broadcasted_iota(jnp.int32, (STATS, value_t.shape[1]), 0)
            ones = jnp.where(row == 0, 1.0, 0.0).astype(jnp.bfloat16)
            value_t = jnp.concatenate([value_t, ones], axis=0)
            summed = lax.dot(value_t, weights.astype(jnp.bfloat16), preferred_element_type=jnp.float32)
            acc_ref[at] += summed[:HEAD]
            l_ref[at] += summed[HEAD : HEAD + 1]
            return
        scores = per_head(allowed, scores, MASKED)
        old = m_ref[at]
        new = jnp.maximum(old, jnp.max(scores, axis=0, keepdims=True) * SCALE)
        weights = jnp.exp2(scores * SCALE - new)
        factor = jnp.exp2(old - new)
        m_ref[at] = new
        l_ref[at] = l_ref[at] * factor + jnp.sum(weights, axis=0, keepdims=True)
        acc_ref[at] = acc_ref[at] * factor + lax.dot(
            value_t, weights.astype(jnp.bfloat16), preferred_element_type=jnp.float32
        )

    def one(src, carry):
        found = []
        for flip, kind, blocks in tiles:
            places = [place(cd, flip, kind, src, j) for j in range(4)]
            low = functools.reduce(jnp.minimum, places)
            high = functools.reduce(jnp.maximum, places) + (TOKENS - 1)
            active = (high >= start_first) & (low <= q_first + (TOKENS - 1))
            whole = active & (high <= q_first) & (low >= start_last) & safe
            found.append((blocks, places, active, whole))
        together = False
        if len(found) == 2:
            together = found[0][3] & found[1][3]

            @pl.when(together)
            def _():
                visit(src, found[0][0] + found[1][0], None, False, False)

        for blocks, places, active, whole in found:

            @pl.when(whole & jnp.logical_not(together))
            def _(blocks=blocks, places=places):
                visit(src, blocks, places, False, False)

            @pl.when(active & jnp.logical_not(whole) & safe)
            def _(blocks=blocks, places=places):
                visit(src, blocks, places, True, False)

            @pl.when(active & jnp.logical_not(safe))
            def _(blocks=blocks, places=places):
                visit(src, blocks, places, True, True)

        return carry

    lax.fori_loop(0, 2, one, 0)


def tiles_of(kinds, refs):
    out, at = [], 0
    for flip, names, shared in kinds:
        each = 4 // shared
        for i, name in enumerate(names):
            out.append((flip, name, [(refs[at + k], each * i + j) for k in range(shared) for j in range(each)]))
        at += shared
    return out


def own_kernel(kinds, n, cd, lengths, *refs):
    tiles, rest = tiles_of(kinds, refs), refs[n:]
    a_ref, b_ref, c_ref, info, qt_ref, m_ref, l_ref, acc_ref = rest
    qt_ref[0] = a_ref[...]
    qt_ref[1] = b_ref[...]
    qt_ref[2:] = c_ref[...]

    def one(qi, carry):
        rows = qt_ref[qi, HEAD:].astype(jnp.float32)
        unsafe = (jnp.max(rows[2:3]) > 0.5).astype(jnp.int32)
        q_first = first_of(cd, qi)
        info[4 * qi] = q_first
        info[4 * qi + 1] = start_of(lengths, q_first)
        info[4 * qi + 2] = start_of(lengths, q_first + (TOKENS - 1))
        info[4 * qi + 3] = unsafe
        m_ref[qi] = jnp.where(unsafe == 0, rows[0:1] + rows[1:2], LOWEST)
        l_ref[qi] = jnp.zeros_like(l_ref[qi])
        acc_ref[qi] = jnp.zeros_like(acc_ref[qi])
        fold(cd, lengths, info, tiles, qi, qt_ref, qi, m_ref, l_ref, acc_ref)
        return carry

    lax.fori_loop(0, 4, one, 0)


def part_kernel(kinds, n, cd, lengths, info, *refs):
    tiles, (qt_ref, *state, m_ref, l_ref, acc_ref) = tiles_of(kinds, refs), refs[n:]

    def one(qi, carry):
        m_ref[qi], l_ref[qi], acc_ref[qi] = (r[qi] for r in state)
        fold(cd, lengths, info, tiles, qi, qt_ref, qi, m_ref, l_ref, acc_ref)
        return carry

    lax.fori_loop(0, 4, one, 0)


def last_kernel(kinds, n, qis, cd, lengths, info, *refs):
    tiles, (qt_ref, *state) = tiles_of(kinds, refs), refs[n : n + 4]
    *out_refs, m_ref, l_ref, acc_ref = refs[n + 4 :]
    for qi, out_ref in zip(qis, out_refs):
        m_ref[0], l_ref[0], acc_ref[0] = (r[qi] for r in state)
        fold(cd, lengths, info, tiles, qi, qt_ref, 0, m_ref, l_ref, acc_ref)
        high, low = halves(m_ref[0])
        factor = jnp.exp2(m_ref[0] - (high + low))
        out_ref[:HEAD] = (acc_ref[0] * factor).astype(jnp.bfloat16)
        row = lax.broadcasted_iota(jnp.int32, (STATS, ROWS), 0)
        out_ref[HEAD:] = stacked(row, high, low, *halves(l_ref[0] * factor))


def unpacked(ref):
    stats = ref[HEAD:].astype(jnp.float32)
    return stats[0:1] + stats[1:2], stats[2:3] + stats[3:4], ref[:HEAD]


def final_kernel(kinds, n, cd, lengths, info, *refs):
    tiles, (qt_ref, packed_ref, *state) = tiles_of(kinds, refs), refs[n : n + 5]
    m_ref, l_ref, acc_ref = refs[n + 5 :]
    m_ref[0], l_ref[0], acc_ref[0] = (r[0] for r in state)
    fold(cd, lengths, info, tiles, 0, qt_ref, 0, m_ref, l_ref, acc_ref)
    m_a, l_a, acc_a = unpacked(packed_ref)
    m_b = m_ref[0]
    top = jnp.maximum(m_a, m_b)
    f_a, f_b = jnp.exp2(m_a - top), jnp.exp2(m_b - top)
    m_ref[0] = top
    l_ref[0] = l_a * f_a + l_ref[0] * f_b
    acc_ref[0] = acc_a.astype(jnp.float32) * f_a + acc_ref[0] * f_b


def combine_kernel(a_ref, b_ref, m_ref, l_ref, acc_ref, out_ref):
    states = [unpacked(a_ref), unpacked(b_ref), (m_ref[0], l_ref[0], acc_ref[0])]
    top = functools.reduce(jnp.maximum, [m for m, _, _ in states])
    factors = [jnp.exp2(m - top) for m, _, _ in states]
    total = sum(f * l for f, (_, l, _) in zip(factors, states))
    inverse = [f / total for f in factors]
    for h in range(HEADS):
        s = slice(h * TOKENS, (h + 1) * TOKENS)
        summed = sum(i[:, s] * acc[:, s].astype(jnp.float32) for i, (_, _, acc) in zip(inverse, states))
        out_ref[:, s] = summed.T.astype(jnp.bfloat16)


VMEM = pl.BlockSpec(memory_space=pltpu.VMEM)
SMEM = pl.BlockSpec(memory_space=pltpu.SMEM)
LONG = 2**13
STATE = [
    jax.ShapeDtypeStruct((4, 1, ROWS), jnp.float32),
    jax.ShapeDtypeStruct((4, 1, ROWS), jnp.float32),
    jax.ShapeDtypeStruct((4, HEAD, ROWS), jnp.float32),
]
PACKED = jax.ShapeDtypeStruct((HEAD + STATS, ROWS), jnp.bfloat16)
SCRATCH = [
    pltpu.VMEM((1, 1, ROWS), jnp.float32),
    pltpu.VMEM((1, 1, ROWS), jnp.float32),
    pltpu.VMEM((1, HEAD, ROWS), jnp.float32),
]


def call(kernel, name, out_shape, scalars, arrays, out_specs, cost=1, scratch=()):
    return pl.pallas_call(
        kernel,
        out_shape=out_shape,
        in_specs=[SMEM] * len(scalars) + [VMEM] * len(arrays),
        out_specs=out_specs,
        scratch_shapes=list(scratch),
        compiler_params=pltpu.CompilerParams(vmem_limit_bytes=16 * 2**20),
        cost_estimate=pl.CostEstimate(
            flops=cost * 2**20, bytes_accessed=cost * 2**10, transcendentals=cost * 2**10
        ),
        name=name,
    )(*scalars, *arrays)


def join(*arrays, cost=1):
    shape = (sum(a.shape[0] for a in arrays), *arrays[0].shape[1:])
    return call(join_kernel, "join", jax.ShapeDtypeStruct(shape, jnp.bfloat16), (), arrays, VMEM, cost)


def shards(queries, keys, values, lengths):
    cd = (lax.axis_index("inner") * 32 + lax.axis_index("outer")).astype(jnp.int32).reshape(1)
    scalars = (cd, lengths)

    def to_slot(s):
        return lambda xp, zp, **_: dict(xp=xp ^ (s // 2), zp=zp ^ (s % 2))

    def swap(x):
        return move(x, lambda c, **_: dict(c=1 - c))

    raw = jnp.stack([keys, values])
    qt = pl.pallas_call(prep_kernel, out_shape=PACKED, in_specs=[VMEM] * 2, out_specs=VMEM, name="prep")(
        queries, keys
    )
    with jax.named_scope("queries_z"):
        qz = move(qt, to_slot(1))

    with jax.named_scope("keys_x"):
        before = move(raw, to_next_span)
        mine = move(raw, lambda xp, y, **_: dict(xp=xp ^ (y & 1)))
    with jax.named_scope("keys_z1"):
        shape = jax.ShapeDtypeStruct((1, 2, 2, TOKENS, HEAD), jnp.bfloat16)
        held = call(pair_kernel, "pair", shape, (), [mine, before], VMEM, LONG)
        got = move(held, lambda w, c, **_: dict(w=w ^ (1 if c else 2)))
    with jax.named_scope("queries_x"):
        qx = move(jnp.stack([qt, qz]), to_slot(2))
    def along_y1(x):
        return move(x, lambda y, c, **_: dict(y=3 - y if c else y ^ 1))

    def along_y2(x):
        return move(x, lambda y, c, **_: dict(y=y ^ 1 if c else 3 - y))

    with jax.named_scope("keys_z2"):
        half = join(held, got)
        rest = move(half, lambda w, c, **_: dict(w=w ^ (2 if c else 1)))
    with jax.named_scope("keys_y1"):
        one_half = along_y1(half)
        held = join(half, rest, cost=LONG)
        rest, held, one_half = lax.optimization_barrier((rest, held, one_half))
        one_rest = along_y1(rest)
    with jax.named_scope("keys_y2"):
        far_half = along_y2(join(half, one_half))

    info, q4, *state = call(
        functools.partial(own_kernel, [(0, ["own"], 1)], 1),
        "own",
        [jax.ShapeDtypeStruct((16,), jnp.int32), jax.ShapeDtypeStruct((4, *PACKED.shape), jnp.bfloat16)] + STATE,
        scalars,
        [held, qt, qz, qx],
        [SMEM] + [VMEM] * 4,
    )
    scalars = (cd, lengths, info)

    def part(name, kinds, arrays, state):
        kernel = functools.partial(part_kernel, kinds, len(arrays))
        return call(kernel, name, STATE, scalars, [*arrays, q4, *state], [VMEM] * 3)

    one_rest, far_half, state = lax.optimization_barrier((one_rest, far_half, state))
    with jax.named_scope("keys_y2"):
        far_rest = along_y2(join(rest, one_rest))
    one = join(one_half, one_rest)
    with jax.named_scope("keys_c1"):
        held_o = swap(held)
        one_o = swap(one)
        far_half_o = swap(far_half)
    state = part("one", [(0, ["one"], 1)], [one], state)
    state = part("other", [(1, ["own"], 1), (1, ["one"], 1)], [held_o, one_o], state)
    far_rest, far_half_o, state = lax.optimization_barrier((far_rest, far_half_o, state))
    with jax.named_scope("keys_c2"):
        far_rest_o = swap(far_rest)
    state = part("far", [(0, ["two", "far"], 2)], [far_half, far_rest], state)
    kinds = [(1, ["two", "far"], 2)]
    far_o = [far_half_o, far_rest_o]
    sent = {}
    for qis in ((3,), (2, 1)):
        kernel = functools.partial(last_kernel, kinds, 2, qis)
        packed = call(
            kernel, "last", [PACKED] * len(qis), scalars, [*far_o, q4, *state], [VMEM] * len(qis), 1, SCRATCH
        )
        packed, state = lax.optimization_barrier((packed, state))
        sent.update(zip(qis, packed))
    with jax.named_scope("sums"):
        got = {s: move(sent[s], to_slot(s)) for s in (3, 2, 1)}
    shape = [jax.ShapeDtypeStruct((1, *x.shape[1:]), x.dtype) for x in STATE]
    kernel = functools.partial(final_kernel, kinds, 2)
    state = call(kernel, "final", shape, scalars, [*far_o, q4, got[3], *state], [VMEM] * 3, LONG)
    out_shape = jax.ShapeDtypeStruct((TOKENS, ROWS), jnp.bfloat16)
    return call(combine_kernel, "combine", out_shape, (), [got[2], got[1], *state], VMEM)


def solution(mesh):
    spec = P(AXES, None)
    return jax.shard_map(shards, mesh=mesh, in_specs=(spec, spec, spec, P()), out_specs=spec, check_vma=False)
```

```python
import functools
import math

import jax
import jax.numpy as jnp
from jax import lax
from jax.experimental import pallas as pl
from jax.experimental.pallas import tpu as pltpu
from jax.sharding import PartitionSpec as P

AXES = ("inner", "outer")
HEAD = 128
HEADS = 8
TOKENS = 128
DOCS = 16
ROWS = HEADS * TOKENS
SPAN = 16384
SCALE = HEAD**-0.5 * math.log2(math.e)
ROOM = 50.0
LARGEST_KEY = 6.0
HEADROOM = 100.0
LOWEST = -float(2**66)
MASKED = -1e30
STATS = 16


def coords(i):
    inner, outer = divmod(i, 32)
    return dict(zh=inner // 8, u=inner // 4 % 2, xp=inner // 2 % 2, c=inner % 2, y=outer // 8, w=outer // 2 % 4, zp=outer % 2)


def index(d):
    inner = d["zh"] * 8 + d["u"] * 4 + d["xp"] * 2 + d["c"]
    return inner * 32 + d["y"] * 8 + d["w"] * 2 + d["zp"]


def move(x, f):
    pairs = []
    for i in range(512):
        d = coords(i)
        to = f(**d)
        if to is not None:
            pairs.append((i, index({**d, **to})))
    return lax.ppermute(x, AXES, pairs)


def to_next_span(zh, u, xp, y, w, **_):
    span = 2 * zh + u + 1
    if span > 3:
        return None
    return dict(zh=span // 2, u=span % 2, xp=xp ^ (y & 1), w=3 - w if span == 2 else w)


def halves(x):
    high = x.astype(jnp.bfloat16).astype(jnp.float32)
    return high, (x - high).astype(jnp.bfloat16).astype(jnp.float32)


def stacked(row, *rows):
    out = jnp.zeros(row.shape, jnp.float32)
    for i, x in enumerate(rows):
        out = jnp.where(row == i, x, out)
    return out.astype(jnp.bfloat16)


def prep_kernel(q_ref, k_ref, o_ref):
    key_t = k_ref[...].T.astype(jnp.float32)
    row = lax.broadcasted_iota(jnp.int32, (STATS, TOKENS), 0)
    for h in range(HEADS):
        s = slice(h * HEAD, (h + 1) * HEAD)
        query_t = q_ref[:, s].T
        o_ref[:HEAD, s] = query_t
        query = query_t.astype(jnp.float32)
        shift = jnp.sum(query * key_t, axis=0, keepdims=True) * SCALE + ROOM
        high, low = halves(shift)
        highest = jnp.sum(jnp.abs(query), axis=0, keepdims=True) * (LARGEST_KEY * SCALE)
        unsafe = jnp.where(highest - shift > HEADROOM, 1.0, 0.0)
        o_ref[HEAD:, s] = stacked(row, high, low, unsafe)


def pair_kernel(a_ref, b_ref, out_ref):
    for i, ref in enumerate((a_ref, b_ref)):
        out_ref[0, i, 0] = ref[0]
        out_ref[0, i, 1] = ref[1].T


def join_kernel(*refs):
    *in_refs, out_ref = refs
    at = 0
    for ref in in_refs:
        out_ref[at : at + ref.shape[0]] = ref[...]
        at += ref.shape[0]


def near(y, cc):
    return jnp.where(cc == 0, y ^ 1, 3 - y)


def place_of(cd):
    me = cd[0]
    return me >> 7, (me >> 6) & 1, (me >> 5) & 1, (me >> 3) & 3, (me >> 1) & 3, me & 1


def place(cd, flip, kind, src, slot):
    span, xp, c, y, w, zp = place_of(cd)
    cc = c ^ flip
    yy = {"own": y, "one": near(y, cc), "two": near(y, 1 - cc), "far": (y + 2) & 3}[kind]
    ww = w ^ jnp.where(cc == 0, (0, 2, 1, 3)[slot], slot)
    ww = jnp.where((src == 1) & (span == 2), 3 - ww, ww)
    return SPAN * (span - src) + 8192 * (xp ^ (yy & 1)) + 4096 * cc + 1024 * yy + 256 * ww + 128 * zp


def first_of(cd, qi):
    span, xp, c, y, w, zp = place_of(cd)
    return SPAN * span + 8192 * (xp ^ (qi >> 1)) + 4096 * c + 1024 * y + 256 * w + 128 * (zp ^ (qi & 1))


def start_of(lengths, positions):
    end, start = jnp.int32(0), jnp.zeros_like(positions)
    for d in range(DOCS):
        end = end + lengths[d]
        start = jnp.where(end <= positions, end, start)
    return start


def per_head(allowed, x, other):
    return jnp.concatenate(
        [jnp.where(allowed, x[:, h * TOKENS : (h + 1) * TOKENS], other) for h in range(HEADS)], axis=1
    )


def fold(cd, lengths, info, tiles, qi, qt_ref, at, m_ref, l_ref, acc_ref):
    q_first, start_first, start_last, unsafe = (info[4 * qi + j] for j in range(4))
    safe = unsafe == 0

    def visit(src, blocks, places, masked, online):
        key = jnp.concatenate([ref[j, src, 0] for ref, j in blocks], axis=0)
        value_t = jnp.concatenate([ref[j, src, 1] for ref, j in blocks], axis=1)
        if masked:
            iota = lax.broadcasted_iota(jnp.int32, (TOKENS, TOKENS), 0)
            key_pos = jnp.concatenate([iota + p for p in places], axis=0)
            query_pos = q_first + lax.broadcasted_iota(jnp.int32, (1, TOKENS), 1)
            allowed = (key_pos <= query_pos) & (key_pos >= start_of(lengths, query_pos))
        scores = lax.dot(key, qt_ref[qi, :HEAD], preferred_element_type=jnp.float32)
        if not online:
            weights = jnp.exp2(scores * SCALE - m_ref[at])
            if masked:
                weights = per_head(allowed, weights, 0.0)
            row = lax.broadcasted_iota(jnp.int32, (STATS, value_t.shape[1]), 0)
            ones = jnp.where(row == 0, 1.0, 0.0).astype(jnp.bfloat16)
            value_t = jnp.concatenate([value_t, ones], axis=0)
            summed = lax.dot(value_t, weights.astype(jnp.bfloat16), preferred_element_type=jnp.float32)
            acc_ref[at] += summed[:HEAD]
            l_ref[at] += summed[HEAD : HEAD + 1]
            return
        scores = per_head(allowed, scores, MASKED)
        old = m_ref[at]
        new = jnp.maximum(old, jnp.max(scores, axis=0, keepdims=True) * SCALE)
        weights = jnp.exp2(scores * SCALE - new)
        factor = jnp.exp2(old - new)
        m_ref[at] = new
        l_ref[at] = l_ref[at] * factor + jnp.sum(weights, axis=0, keepdims=True)
        acc_ref[at] = acc_ref[at] * factor + lax.dot(
            value_t, weights.astype(jnp.bfloat16), preferred_element_type=jnp.float32
        )

    def one(src, carry):
        found = []
        for flip, kind, blocks in tiles:
            places = [place(cd, flip, kind, src, j) for j in range(4)]
            low = functools.reduce(jnp.minimum, places)
            high = functools.reduce(jnp.maximum, places) + (TOKENS - 1)
            active = (high >= start_first) & (low <= q_first + (TOKENS - 1))
            whole = active & (high <= q_first) & (low >= start_last) & safe
            found.append((blocks, places, active, whole))
        together = False
        if len(found) == 2:
            together = found[0][3] & found[1][3]

            @pl.when(together)
            def _():
                visit(src, found[0][0] + found[1][0], None, False, False)

        for blocks, places, active, whole in found:

            @pl.when(whole & jnp.logical_not(together))
            def _(blocks=blocks, places=places):
                visit(src, blocks, places, False, False)

            @pl.when(active & jnp.logical_not(whole) & safe)
            def _(blocks=blocks, places=places):
                visit(src, blocks, places, True, False)

            @pl.when(active & jnp.logical_not(safe))
            def _(blocks=blocks, places=places):
                visit(src, blocks, places, True, True)

        return carry

    lax.fori_loop(0, 2, one, 0)


def tiles_of(kinds, refs):
    out, at = [], 0
    for flip, names, shared in kinds:
        each = 4 // shared
        for i, name in enumerate(names):
            out.append((flip, name, [(refs[at + k], each * i + j) for k in range(shared) for j in range(each)]))
        at += shared
    return out


def own_kernel(kinds, n, cd, lengths, *refs):
    tiles, rest = tiles_of(kinds, refs), refs[n:]
    a_ref, b_ref, c_ref, info, qt_ref, m_ref, l_ref, acc_ref = rest
    qt_ref[0] = a_ref[...]
    qt_ref[1] = b_ref[...]
    qt_ref[2:] = c_ref[...]

    def one(qi, carry):
        rows = qt_ref[qi, HEAD:].astype(jnp.float32)
        unsafe = (jnp.max(rows[2:3]) > 0.5).astype(jnp.int32)
        q_first = first_of(cd, qi)
        info[4 * qi] = q_first
        info[4 * qi + 1] = start_of(lengths, q_first)
        info[4 * qi + 2] = start_of(lengths, q_first + (TOKENS - 1))
        info[4 * qi + 3] = unsafe
        m_ref[qi] = jnp.where(unsafe == 0, rows[0:1] + rows[1:2], LOWEST)
        l_ref[qi] = jnp.zeros_like(l_ref[qi])
        acc_ref[qi] = jnp.zeros_like(acc_ref[qi])
        fold(cd, lengths, info, tiles, qi, qt_ref, qi, m_ref, l_ref, acc_ref)
        return carry

    lax.fori_loop(0, 4, one, 0)


def part_kernel(kinds, n, cd, lengths, info, *refs):
    tiles, (qt_ref, *state, m_ref, l_ref, acc_ref) = tiles_of(kinds, refs), refs[n:]

    def one(qi, carry):
        m_ref[qi], l_ref[qi], acc_ref[qi] = (r[qi] for r in state)
        fold(cd, lengths, info, tiles, qi, qt_ref, qi, m_ref, l_ref, acc_ref)
        return carry

    lax.fori_loop(0, 4, one, 0)


def last_kernel(kinds, n, qis, cd, lengths, info, *refs):
    tiles, (qt_ref, *state) = tiles_of(kinds, refs), refs[n : n + 4]
    *out_refs, m_ref, l_ref, acc_ref = refs[n + 4 :]
    for qi, out_ref in zip(qis, out_refs):
        m_ref[0], l_ref[0], acc_ref[0] = (r[qi] for r in state)
        fold(cd, lengths, info, tiles, qi, qt_ref, 0, m_ref, l_ref, acc_ref)
        high, low = halves(m_ref[0])
        factor = jnp.exp2(m_ref[0] - (high + low))
        out_ref[:HEAD] = (acc_ref[0] * factor).astype(jnp.bfloat16)
        row = lax.broadcasted_iota(jnp.int32, (STATS, ROWS), 0)
        out_ref[HEAD:] = stacked(row, high, low, *halves(l_ref[0] * factor))


def unpacked(ref):
    stats = ref[HEAD:].astype(jnp.float32)
    return stats[0:1] + stats[1:2], stats[2:3] + stats[3:4], ref[:HEAD]


def final_kernel(kinds, n, cd, lengths, info, *refs):
    tiles, (qt_ref, packed_ref, *state) = tiles_of(kinds, refs), refs[n : n + 5]
    m_ref, l_ref, acc_ref = refs[n + 5 :]
    m_ref[0], l_ref[0], acc_ref[0] = (r[0] for r in state)
    fold(cd, lengths, info, tiles, 0, qt_ref, 0, m_ref, l_ref, acc_ref)
    m_a, l_a, acc_a = unpacked(packed_ref)
    m_b = m_ref[0]
    top = jnp.maximum(m_a, m_b)
    f_a, f_b = jnp.exp2(m_a - top), jnp.exp2(m_b - top)
    m_ref[0] = top
    l_ref[0] = l_a * f_a + l_ref[0] * f_b
    acc_ref[0] = acc_a.astype(jnp.float32) * f_a + acc_ref[0] * f_b


def combine_kernel(a_ref, b_ref, m_ref, l_ref, acc_ref, out_ref):
    states = [unpacked(a_ref), unpacked(b_ref), (m_ref[0], l_ref[0], acc_ref[0])]
    top = functools.reduce(jnp.maximum, [m for m, _, _ in states])
    factors = [jnp.exp2(m - top) for m, _, _ in states]
    total = sum(f * l for f, (_, l, _) in zip(factors, states))
    inverse = [f / total for f in factors]
    for h in range(HEADS):
        s = slice(h * TOKENS, (h + 1) * TOKENS)
        summed = sum(i[:, s] * acc[:, s].astype(jnp.float32) for i, (_, _, acc) in zip(inverse, states))
        out_ref[:, s] = summed.T.astype(jnp.bfloat16)


VMEM = pl.BlockSpec(memory_space=pltpu.VMEM)
SMEM = pl.BlockSpec(memory_space=pltpu.SMEM)
LONG = 2**13
STATE = [
    jax.ShapeDtypeStruct((4, 1, ROWS), jnp.float32),
    jax.ShapeDtypeStruct((4, 1, ROWS), jnp.float32),
    jax.ShapeDtypeStruct((4, HEAD, ROWS), jnp.float32),
]
PACKED = jax.ShapeDtypeStruct((HEAD + STATS, ROWS), jnp.bfloat16)
SCRATCH = [
    pltpu.VMEM((1, 1, ROWS), jnp.float32),
    pltpu.VMEM((1, 1, ROWS), jnp.float32),
    pltpu.VMEM((1, HEAD, ROWS), jnp.float32),
]


def call(kernel, name, out_shape, scalars, arrays, out_specs, cost=1, scratch=()):
    return pl.pallas_call(
        kernel,
        out_shape=out_shape,
        in_specs=[SMEM] * len(scalars) + [VMEM] * len(arrays),
        out_specs=out_specs,
        scratch_shapes=list(scratch),
        compiler_params=pltpu.CompilerParams(vmem_limit_bytes=16 * 2**20),
        cost_estimate=pl.CostEstimate(
            flops=cost * 2**20, bytes_accessed=cost * 2**10, transcendentals=cost * 2**10
        ),
        name=name,
    )(*scalars, *arrays)


def join(*arrays, cost=1):
    shape = (sum(a.shape[0] for a in arrays), *arrays[0].shape[1:])
    return call(join_kernel, "join", jax.ShapeDtypeStruct(shape, jnp.bfloat16), (), arrays, VMEM, cost)


def shards(queries, keys, values, lengths):
    cd = (lax.axis_index("inner") * 32 + lax.axis_index("outer")).astype(jnp.int32).reshape(1)
    scalars = (cd, lengths)

    def to_slot(s):
        return lambda xp, zp, **_: dict(xp=xp ^ (s // 2), zp=zp ^ (s % 2))

    def swap(x):
        return move(x, lambda c, **_: dict(c=1 - c))

    raw = jnp.stack([keys, values])
    qt = pl.pallas_call(prep_kernel, out_shape=PACKED, in_specs=[VMEM] * 2, out_specs=VMEM, name="prep")(
        queries, keys
    )

    with jax.named_scope("keys_x"):
        before = move(raw, to_next_span)
        mine = move(raw, lambda xp, y, **_: dict(xp=xp ^ (y & 1)))
        mine, before, qt = lax.optimization_barrier((mine, before, qt))
    with jax.named_scope("queries_z"):
        qz = move(qt, to_slot(1))
    with jax.named_scope("keys_z1"):
        shape = jax.ShapeDtypeStruct((1, 2, 2, TOKENS, HEAD), jnp.bfloat16)
        held = call(pair_kernel, "pair", shape, (), [mine, before], VMEM, LONG)
        got = move(held, lambda w, c, **_: dict(w=w ^ (1 if c else 2)))
    with jax.named_scope("queries_x"):
        qx = move(jnp.stack([qt, qz]), to_slot(2))
    def along_y1(x):
        return move(x, lambda y, c, **_: dict(y=3 - y if c else y ^ 1))

    def along_y2(x):
        return move(x, lambda y, c, **_: dict(y=y ^ 1 if c else 3 - y))

    with jax.named_scope("keys_z2"):
        half = join(held, got, cost=LONG)
        rest = move(half, lambda w, c, **_: dict(w=w ^ (2 if c else 1)))
    with jax.named_scope("keys_y1"):
        one_half = along_y1(half)
        held = join(half, rest, cost=LONG)
        rest, held, one_half = lax.optimization_barrier((rest, held, one_half))
        one_rest = along_y1(rest)
    with jax.named_scope("keys_y2"):
        far_half = along_y2(join(half, one_half))

    info, q4, *state = call(
        functools.partial(own_kernel, [(0, ["own"], 1)], 1),
        "own",
        [jax.ShapeDtypeStruct((16,), jnp.int32), jax.ShapeDtypeStruct((4, *PACKED.shape), jnp.bfloat16)] + STATE,
        scalars,
        [held, qt, qz, qx],
        [SMEM] + [VMEM] * 4,
    )
    scalars = (cd, lengths, info)

    def part(name, kinds, arrays, state):
        kernel = functools.partial(part_kernel, kinds, len(arrays))
        return call(kernel, name, STATE, scalars, [*arrays, q4, *state], [VMEM] * 3)

    one_rest, far_half, state = lax.optimization_barrier((one_rest, far_half, state))
    with jax.named_scope("keys_y2"):
        far_rest = along_y2(join(rest, one_rest))
    one = join(one_half, one_rest)
    with jax.named_scope("keys_c1"):
        held_o = swap(held)
        one_o = swap(one)
        far_half_o = swap(far_half)
    state = part("one", [(0, ["one"], 1)], [one], state)
    state = part("other", [(1, ["own"], 1), (1, ["one"], 1)], [held_o, one_o], state)
    far_rest, far_half_o, state = lax.optimization_barrier((far_rest, far_half_o, state))
    with jax.named_scope("keys_c2"):
        far_rest_o = swap(far_rest)
    state = part("far", [(0, ["two", "far"], 2)], [far_half, far_rest], state)
    kinds = [(1, ["two", "far"], 2)]
    far_o = [far_half_o, far_rest_o]
    sent = {}
    for qis in ((3,), (2, 1)):
        kernel = functools.partial(last_kernel, kinds, 2, qis)
        packed = call(
            kernel, "last", [PACKED] * len(qis), scalars, [*far_o, q4, *state], [VMEM] * len(qis), 1, SCRATCH
        )
        packed, state = lax.optimization_barrier((packed, state))
        sent.update(zip(qis, packed))
    with jax.named_scope("sums"):
        got = {s: move(sent[s], to_slot(s)) for s in (3, 2, 1)}
    shape = [jax.ShapeDtypeStruct((1, *x.shape[1:]), x.dtype) for x in STATE]
    kernel = functools.partial(final_kernel, kinds, 2)
    state = call(kernel, "final", shape, scalars, [*far_o, q4, got[3], *state], [VMEM] * 3, LONG)
    out_shape = jax.ShapeDtypeStruct((TOKENS, ROWS), jnp.bfloat16)
    return call(combine_kernel, "combine", out_shape, (), [got[2], got[1], *state], VMEM)


def solution(mesh):
    spec = P(AXES, None)
    return jax.shard_map(shards, mesh=mesh, in_specs=(spec, spec, spec, P()), out_specs=spec, check_vma=False)
```

```python
import functools
import math

import jax
import jax.numpy as jnp
from jax import lax
from jax.experimental import pallas as pl
from jax.experimental.pallas import tpu as pltpu
from jax.sharding import PartitionSpec as P

AXES = ("inner", "outer")
HEAD = 128
HEADS = 8
TOKENS = 128
DOCS = 16
ROWS = HEADS * TOKENS
SPAN = 16384
SCALE = HEAD**-0.5 * math.log2(math.e)
ROOM = 50.0
LARGEST_KEY = 6.0
HEADROOM = 100.0
LOWEST = -float(2**66)
MASKED = -1e30
STATS = 16


def coords(i):
    inner, outer = divmod(i, 32)
    return dict(zh=inner // 8, u=inner // 4 % 2, xp=inner // 2 % 2, c=inner % 2, y=outer // 8, w=outer // 2 % 4, zp=outer % 2)


def index(d):
    inner = d["zh"] * 8 + d["u"] * 4 + d["xp"] * 2 + d["c"]
    return inner * 32 + d["y"] * 8 + d["w"] * 2 + d["zp"]


def move(x, f):
    pairs = []
    for i in range(512):
        d = coords(i)
        to = f(**d)
        if to is not None:
            pairs.append((i, index({**d, **to})))
    return lax.ppermute(x, AXES, pairs)


def to_next_span(zh, u, xp, y, w, **_):
    span = 2 * zh + u + 1
    if span > 3:
        return None
    return dict(zh=span // 2, u=span % 2, xp=xp ^ (y & 1), w=3 - w if span == 2 else w)


def halves(x):
    high = x.astype(jnp.bfloat16).astype(jnp.float32)
    return high, (x - high).astype(jnp.bfloat16).astype(jnp.float32)


def stacked(row, *rows):
    out = jnp.zeros(row.shape, jnp.float32)
    for i, x in enumerate(rows):
        out = jnp.where(row == i, x, out)
    return out.astype(jnp.bfloat16)


def prep_kernel(q_ref, k_ref, o_ref):
    key_t = k_ref[...].T.astype(jnp.float32)
    row = lax.broadcasted_iota(jnp.int32, (STATS, TOKENS), 0)
    for h in range(HEADS):
        s = slice(h * HEAD, (h + 1) * HEAD)
        query_t = q_ref[:, s].T
        o_ref[:HEAD, s] = query_t
        query = query_t.astype(jnp.float32)
        shift = jnp.sum(query * key_t, axis=0, keepdims=True) * SCALE + ROOM
        high, low = halves(shift)
        highest = jnp.sum(jnp.abs(query), axis=0, keepdims=True) * (LARGEST_KEY * SCALE)
        unsafe = jnp.where(highest - shift > HEADROOM, 1.0, 0.0)
        o_ref[HEAD:, s] = stacked(row, high, low, unsafe)


def pair_kernel(a_ref, b_ref, out_ref):
    for i, ref in enumerate((a_ref, b_ref)):
        out_ref[0, i, 0] = ref[0]
        out_ref[0, i, 1] = ref[1].T


def join_kernel(*refs):
    *in_refs, out_ref = refs
    at = 0
    for ref in in_refs:
        out_ref[at : at + ref.shape[0]] = ref[...]
        at += ref.shape[0]


def near(y, cc):
    return jnp.where(cc == 0, y ^ 1, 3 - y)


def place_of(cd):
    me = cd[0]
    return me >> 7, (me >> 6) & 1, (me >> 5) & 1, (me >> 3) & 3, (me >> 1) & 3, me & 1


def place(cd, flip, kind, src, slot):
    span, xp, c, y, w, zp = place_of(cd)
    cc = c ^ flip
    yy = {"own": y, "one": near(y, cc), "two": near(y, 1 - cc), "far": (y + 2) & 3}[kind]
    ww = w ^ jnp.where(cc == 0, (0, 2, 1, 3)[slot], slot)
    ww = jnp.where((src == 1) & (span == 2), 3 - ww, ww)
    return SPAN * (span - src) + 8192 * (xp ^ (yy & 1)) + 4096 * cc + 1024 * yy + 256 * ww + 128 * zp


def first_of(cd, qi):
    span, xp, c, y, w, zp = place_of(cd)
    return SPAN * span + 8192 * (xp ^ (qi >> 1)) + 4096 * c + 1024 * y + 256 * w + 128 * (zp ^ (qi & 1))


def start_of(lengths, positions):
    end, start = jnp.int32(0), jnp.zeros_like(positions)
    for d in range(DOCS):
        end = end + lengths[d]
        start = jnp.where(end <= positions, end, start)
    return start


def per_head(allowed, x, other):
    return jnp.concatenate(
        [jnp.where(allowed, x[:, h * TOKENS : (h + 1) * TOKENS], other) for h in range(HEADS)], axis=1
    )


def fold(cd, lengths, info, tiles, qi, qt_ref, at, m_ref, l_ref, acc_ref):
    q_first, start_first, start_last, unsafe = (info[4 * qi + j] for j in range(4))
    safe = unsafe == 0

    def visit(src, blocks, places, masked, online):
        key = jnp.concatenate([ref[j, src, 0] for ref, j in blocks], axis=0)
        value_t = jnp.concatenate([ref[j, src, 1] for ref, j in blocks], axis=1)
        if masked:
            iota = lax.broadcasted_iota(jnp.int32, (TOKENS, TOKENS), 0)
            key_pos = jnp.concatenate([iota + p for p in places], axis=0)
            query_pos = q_first + lax.broadcasted_iota(jnp.int32, (1, TOKENS), 1)
            allowed = (key_pos <= query_pos) & (key_pos >= start_of(lengths, query_pos))
        scores = lax.dot(key, qt_ref[qi, :HEAD], preferred_element_type=jnp.float32)
        if not online:
            weights = jnp.exp2(scores * SCALE - m_ref[at])
            if masked:
                weights = per_head(allowed, weights, 0.0)
            row = lax.broadcasted_iota(jnp.int32, (STATS, value_t.shape[1]), 0)
            ones = jnp.where(row == 0, 1.0, 0.0).astype(jnp.bfloat16)
            value_t = jnp.concatenate([value_t, ones], axis=0)
            summed = lax.dot(value_t, weights.astype(jnp.bfloat16), preferred_element_type=jnp.float32)
            acc_ref[at] += summed[:HEAD]
            l_ref[at] += summed[HEAD : HEAD + 1]
            return
        scores = per_head(allowed, scores, MASKED)
        old = m_ref[at]
        new = jnp.maximum(old, jnp.max(scores, axis=0, keepdims=True) * SCALE)
        weights = jnp.exp2(scores * SCALE - new)
        factor = jnp.exp2(old - new)
        m_ref[at] = new
        l_ref[at] = l_ref[at] * factor + jnp.sum(weights, axis=0, keepdims=True)
        acc_ref[at] = acc_ref[at] * factor + lax.dot(
            value_t, weights.astype(jnp.bfloat16), preferred_element_type=jnp.float32
        )

    def one(src, carry):
        found = []
        for flip, kind, blocks in tiles:
            places = [place(cd, flip, kind, src, j) for j in range(4)]
            low = functools.reduce(jnp.minimum, places)
            high = functools.reduce(jnp.maximum, places) + (TOKENS - 1)
            active = (high >= start_first) & (low <= q_first + (TOKENS - 1))
            whole = active & (high <= q_first) & (low >= start_last) & safe
            found.append((blocks, places, active, whole))
        together = False
        if len(found) == 2:
            together = found[0][3] & found[1][3]

            @pl.when(together)
            def _():
                visit(src, found[0][0] + found[1][0], None, False, False)

        for blocks, places, active, whole in found:

            @pl.when(whole & jnp.logical_not(together))
            def _(blocks=blocks, places=places):
                visit(src, blocks, places, False, False)

            @pl.when(active & jnp.logical_not(whole) & safe)
            def _(blocks=blocks, places=places):
                visit(src, blocks, places, True, False)

            @pl.when(active & jnp.logical_not(safe))
            def _(blocks=blocks, places=places):
                visit(src, blocks, places, True, True)

        return carry

    lax.fori_loop(0, 2, one, 0)


def tiles_of(kinds, refs):
    out, at = [], 0
    for flip, names, shared in kinds:
        each = 4 // shared
        for i, name in enumerate(names):
            out.append((flip, name, [(refs[at + k], each * i + j) for k in range(shared) for j in range(each)]))
        at += shared
    return out


def own_kernel(kinds, n, cd, lengths, *refs):
    tiles, rest = tiles_of(kinds, refs), refs[n:]
    a_ref, b_ref, c_ref, info, qt_ref, m_ref, l_ref, acc_ref = rest
    qt_ref[0] = a_ref[...]
    qt_ref[1] = b_ref[...]
    qt_ref[2:] = c_ref[...]

    def one(qi, carry):
        rows = qt_ref[qi, HEAD:].astype(jnp.float32)
        unsafe = (jnp.max(rows[2:3]) > 0.5).astype(jnp.int32)
        q_first = first_of(cd, qi)
        info[4 * qi] = q_first
        info[4 * qi + 1] = start_of(lengths, q_first)
        info[4 * qi + 2] = start_of(lengths, q_first + (TOKENS - 1))
        info[4 * qi + 3] = unsafe
        m_ref[qi] = jnp.where(unsafe == 0, rows[0:1] + rows[1:2], LOWEST)
        l_ref[qi] = jnp.zeros_like(l_ref[qi])
        acc_ref[qi] = jnp.zeros_like(acc_ref[qi])
        fold(cd, lengths, info, tiles, qi, qt_ref, qi, m_ref, l_ref, acc_ref)
        return carry

    lax.fori_loop(0, 4, one, 0)


def part_kernel(kinds, n, cd, lengths, info, *refs):
    tiles, (qt_ref, *state, m_ref, l_ref, acc_ref) = tiles_of(kinds, refs), refs[n:]

    def one(qi, carry):
        m_ref[qi], l_ref[qi], acc_ref[qi] = (r[qi] for r in state)
        fold(cd, lengths, info, tiles, qi, qt_ref, qi, m_ref, l_ref, acc_ref)
        return carry

    lax.fori_loop(0, 4, one, 0)


def last_kernel(kinds, n, qis, cd, lengths, info, *refs):
    tiles, (qt_ref, *state) = tiles_of(kinds, refs), refs[n : n + 4]
    *out_refs, m_ref, l_ref, acc_ref = refs[n + 4 :]
    for qi, out_ref in zip(qis, out_refs):
        m_ref[0], l_ref[0], acc_ref[0] = (r[qi] for r in state)
        fold(cd, lengths, info, tiles, qi, qt_ref, 0, m_ref, l_ref, acc_ref)
        high, low = halves(m_ref[0])
        factor = jnp.exp2(m_ref[0] - (high + low))
        out_ref[:HEAD] = (acc_ref[0] * factor).astype(jnp.bfloat16)
        row = lax.broadcasted_iota(jnp.int32, (STATS, ROWS), 0)
        out_ref[HEAD:] = stacked(row, high, low, *halves(l_ref[0] * factor))


def unpacked(ref):
    stats = ref[HEAD:].astype(jnp.float32)
    return stats[0:1] + stats[1:2], stats[2:3] + stats[3:4], ref[:HEAD]


def final_kernel(kinds, n, cd, lengths, info, *refs):
    tiles, (qt_ref, a_ref, b_ref, *state) = tiles_of(kinds, refs), refs[n : n + 6]
    m_ref, l_ref, acc_ref = refs[n + 6 :]
    m_ref[0], l_ref[0], acc_ref[0] = (r[0] for r in state)
    fold(cd, lengths, info, tiles, 0, qt_ref, 0, m_ref, l_ref, acc_ref)
    for packed_ref in (a_ref, b_ref):
        m_a, l_a, acc_a = unpacked(packed_ref)
        m_b = m_ref[0]
        top = jnp.maximum(m_a, m_b)
        f_a, f_b = jnp.exp2(m_a - top), jnp.exp2(m_b - top)
        m_ref[0] = top
        l_ref[0] = l_a * f_a + l_ref[0] * f_b
        acc_ref[0] = acc_a.astype(jnp.float32) * f_a + acc_ref[0] * f_b


def combine_kernel(a_ref, m_ref, l_ref, acc_ref, out_ref):
    states = [unpacked(a_ref), (m_ref[0], l_ref[0], acc_ref[0])]
    top = functools.reduce(jnp.maximum, [m for m, _, _ in states])
    factors = [jnp.exp2(m - top) for m, _, _ in states]
    total = sum(f * l for f, (_, l, _) in zip(factors, states))
    inverse = [f / total for f in factors]
    for h in range(HEADS):
        s = slice(h * TOKENS, (h + 1) * TOKENS)
        summed = sum(i[:, s] * acc[:, s].astype(jnp.float32) for i, (_, _, acc) in zip(inverse, states))
        out_ref[:, s] = summed.T.astype(jnp.bfloat16)


VMEM = pl.BlockSpec(memory_space=pltpu.VMEM)
SMEM = pl.BlockSpec(memory_space=pltpu.SMEM)
LONG = 2**13
STATE = [
    jax.ShapeDtypeStruct((4, 1, ROWS), jnp.float32),
    jax.ShapeDtypeStruct((4, 1, ROWS), jnp.float32),
    jax.ShapeDtypeStruct((4, HEAD, ROWS), jnp.float32),
]
PACKED = jax.ShapeDtypeStruct((HEAD + STATS, ROWS), jnp.bfloat16)
SCRATCH = [
    pltpu.VMEM((1, 1, ROWS), jnp.float32),
    pltpu.VMEM((1, 1, ROWS), jnp.float32),
    pltpu.VMEM((1, HEAD, ROWS), jnp.float32),
]


def call(kernel, name, out_shape, scalars, arrays, out_specs, cost=1, scratch=()):
    return pl.pallas_call(
        kernel,
        out_shape=out_shape,
        in_specs=[SMEM] * len(scalars) + [VMEM] * len(arrays),
        out_specs=out_specs,
        scratch_shapes=list(scratch),
        compiler_params=pltpu.CompilerParams(vmem_limit_bytes=16 * 2**20),
        cost_estimate=pl.CostEstimate(
            flops=cost * 2**20, bytes_accessed=cost * 2**10, transcendentals=cost * 2**10
        ),
        name=name,
    )(*scalars, *arrays)


def join(*arrays, cost=1):
    shape = (sum(a.shape[0] for a in arrays), *arrays[0].shape[1:])
    return call(join_kernel, "join", jax.ShapeDtypeStruct(shape, jnp.bfloat16), (), arrays, VMEM, cost)


def shards(queries, keys, values, lengths):
    cd = (lax.axis_index("inner") * 32 + lax.axis_index("outer")).astype(jnp.int32).reshape(1)
    scalars = (cd, lengths)

    def to_slot(s):
        return lambda xp, zp, **_: dict(xp=xp ^ (s // 2), zp=zp ^ (s % 2))

    def swap(x):
        return move(x, lambda c, **_: dict(c=1 - c))

    raw = jnp.stack([keys, values])
    qt = pl.pallas_call(prep_kernel, out_shape=PACKED, in_specs=[VMEM] * 2, out_specs=VMEM, name="prep")(
        queries, keys
    )

    with jax.named_scope("keys_x"):
        before = move(raw, to_next_span)
        mine = move(raw, lambda xp, y, **_: dict(xp=xp ^ (y & 1)))
        mine, before, qt = lax.optimization_barrier((mine, before, qt))
    with jax.named_scope("queries_z"):
        qz = move(qt, to_slot(1))
    with jax.named_scope("keys_z1"):
        shape = jax.ShapeDtypeStruct((1, 2, 2, TOKENS, HEAD), jnp.bfloat16)
        held = call(pair_kernel, "pair", shape, (), [mine, before], VMEM, LONG)
        got = move(held, lambda w, c, **_: dict(w=w ^ (1 if c else 2)))
    with jax.named_scope("queries_x"):
        qx = move(jnp.stack([qt, qz]), to_slot(2))
    def along_y1(x):
        return move(x, lambda y, c, **_: dict(y=3 - y if c else y ^ 1))

    def along_y2(x):
        return move(x, lambda y, c, **_: dict(y=y ^ 1 if c else 3 - y))

    with jax.named_scope("keys_z2"):
        half = join(held, got, cost=LONG)
        rest = move(half, lambda w, c, **_: dict(w=w ^ (2 if c else 1)))
    with jax.named_scope("keys_y1"):
        one_half = along_y1(half)
        held = join(half, rest, cost=LONG)
        rest, held, one_half = lax.optimization_barrier((rest, held, one_half))
        one_rest = along_y1(rest)
    with jax.named_scope("keys_y2"):
        far_half = along_y2(join(half, one_half))

    info, q4, *state = call(
        functools.partial(own_kernel, [(0, ["own"], 1)], 1),
        "own",
        [jax.ShapeDtypeStruct((16,), jnp.int32), jax.ShapeDtypeStruct((4, *PACKED.shape), jnp.bfloat16)] + STATE,
        scalars,
        [held, qt, qz, qx],
        [SMEM] + [VMEM] * 4,
    )
    scalars = (cd, lengths, info)

    def part(name, kinds, arrays, state):
        kernel = functools.partial(part_kernel, kinds, len(arrays))
        return call(kernel, name, STATE, scalars, [*arrays, q4, *state], [VMEM] * 3)

    one_rest, far_half, state = lax.optimization_barrier((one_rest, far_half, state))
    with jax.named_scope("keys_y2"):
        far_rest = along_y2(join(rest, one_rest))
    one = join(one_half, one_rest)
    with jax.named_scope("keys_c1"):
        held_o = swap(held)
        one_o = swap(one)
        far_half_o = swap(far_half)
    state = part("one", [(0, ["one"], 1)], [one], state)
    state = part("other", [(1, ["own"], 1), (1, ["one"], 1)], [held_o, one_o], state)
    far_rest, far_half_o, state = lax.optimization_barrier((far_rest, far_half_o, state))
    with jax.named_scope("keys_c2"):
        far_rest_o = swap(far_rest)
    state = part("far", [(0, ["two", "far"], 2)], [far_half, far_rest], state)
    kinds = [(1, ["two", "far"], 2)]
    far_o = [far_half_o, far_rest_o]
    sent = {}
    for qis in ((3,), (2,), (1,)):
        kernel = functools.partial(last_kernel, kinds, 2, qis)
        packed = call(
            kernel, "last", [PACKED] * len(qis), scalars, [*far_o, q4, *state], [VMEM] * len(qis), 1, SCRATCH
        )
        packed, state = lax.optimization_barrier((packed, state))
        sent.update(zip(qis, packed))
    with jax.named_scope("sums"):
        got = {s: move(sent[s], to_slot(s)) for s in (3, 2, 1)}
    shape = [jax.ShapeDtypeStruct((1, *x.shape[1:]), x.dtype) for x in STATE]
    kernel = functools.partial(final_kernel, kinds, 2)
    state = call(kernel, "final", shape, scalars, [*far_o, q4, got[3], got[2], *state], [VMEM] * 3, LONG)
    out_shape = jax.ShapeDtypeStruct((TOKENS, ROWS), jnp.bfloat16)
    return call(combine_kernel, "combine", out_shape, (), [got[1], *state], VMEM)


def solution(mesh):
    spec = P(AXES, None)
    return jax.shard_map(shards, mesh=mesh, in_specs=(spec, spec, spec, P()), out_specs=spec, check_vma=False)
```
